32 devices in a mesh: len: 2 (over core), wid: 4 (over y, x), hgt: 4 (over z).
Axes of the slice: x: 2, y: 2, z: 4, core: 2. Of those that a mesh axis runs over, the one named last changes fastest.
Arguments:
- e_field: float32 [3, 32, 128, 512], P(None, 'len', 'wid', 'hgt'), may hold values from -6 to 6
- h_field: float32 [3, 32, 128, 512], P(None, 'len', 'wid', 'hgt'), may hold values from -6 to 6
- material: int32 [32, 128, 512], P('len', 'wid', 'hgt'), may hold values from 0 to 15
- permittivity: float32 [16], replicated, may hold values from 1 to 10
- line_volts: float32 [16, 65536], P(None, ('len', 'wid', 'hgt')), may hold values from -6 to 6
- line_amps: float32 [16, 65536], P(None, ('len', 'wid', 'hgt')), may hold values from -6 to 6
- coupling: float32 [16, 65536], P(None, ('len', 'wid', 'hgt')), may hold values from -3 to 3
- seg_brick: int32 [65536], P(('len', 'wid', 'hgt')), may hold values from 0 to 31, as said below
- seg_cell: int32 [65536], P(('len', 'wid', 'hgt')), may hold values from 0 to 65535
- seg_axis: int32 [65536], P(('len', 'wid', 'hgt')), may hold values from 0 to 2
- bundle_type: int32 [65536], P(('len', 'wid', 'hgt')), may hold values from 0 to 7
- path_lengths: int32 [32, 64], P(('len', 'wid', 'hgt')), may hold values from 1 to 64, 2048 in all within a row
- inv_induct: float32 [8, 16, 16], replicated, may hold values from -0.2 to 1.3, as said below
- inv_capac: float32 [8, 16, 16], replicated, may hold values from -0.2 to 1.3, as said below
Outputs:
- e_final: float32 [3, 32, 128, 512], P(None, 'len', 'wid', 'hgt')
- h_final: float32 [3, 32, 128, 512], P(None, 'len', 'wid', 'hgt')
- volts_final: float32 [16, 65536], P(None, ('len', 'wid', 'hgt'))
- amps_final: float32 [16, 65536], P(None, ('len', 'wid', 'hgt'))
The draws below stay inside these ranges and needn't reach their ends.
Inputs may be any that keep to these rules, and one draw needn't show every extreme that they name: `seg_brick`: in each aligned block of 2048 entries (one owner's segments) no brick is named more than 160 times, and in every draw one brick is named exactly 160 times in every block. `inv_induct`: each 16 x 16 block is symmetric. `inv_capac`: each 16 x 16 block is symmetric.
All inputs are finite; a program needn't handle non-finite values.
Results may differ from the reference program's by a relative error of at most 0.0003.
Values sent between devices are 32-bit elements; how exact they have to be, the bound alone decides.
A program may use at most 64 MiB of HBM per device.

```python
import math
import jax
import jax.numpy as jnp
import numpy as np
from jax import lax

COND = 16
BTYPES = 8
MATS = 16
CX = 16
CY = 32
CZ = 128
S_DEV = 2048
NPATH = 64
ITERS = 4
BRICKS = 32
NX = 32
NY = 128
NZ = 512
CELLS = 65536
SEGS = 65536
CAP = 160
PMAX = 64
N_WID = 4
N_HGT = 4


def brick_block(block_key, hot_brick):
    weight_key, rank_key, shuffle_key = jax.random.split(block_key, 3)
    bricks_all = jnp.arange(BRICKS, dtype=jnp.int32)
    weights = jax.random.randint(weight_key, (BRICKS,), 2, 4, dtype=jnp.int32)
    weights = jnp.where(bricks_all == hot_brick, 0, weights)
    remaining = S_DEV - CAP
    counts = (remaining * weights // jnp.sum(weights)).astype(jnp.int32)
    leftover = remaining - jnp.sum(counts)
    ranking = jax.random.permutation(rank_key, BRICKS)
    eligible = (weights > 0).astype(jnp.int32)
    placed = jnp.cumsum(eligible[ranking]).astype(jnp.int32) - 1
    extra_ranked = eligible[ranking] * (placed < leftover).astype(jnp.int32)
    extra_count = jnp.zeros((BRICKS,), jnp.int32).at[ranking].set(extra_ranked)
    counts = jnp.where(bricks_all == hot_brick, CAP, counts + extra_count)
    labels = jnp.repeat(bricks_all, counts, total_repeat_length=S_DEV)
    return labels[jax.random.permutation(shuffle_key, S_DEV)]


def draw_seg_brick(key, part):
    base_key = jax.random.fold_in(key, 303)
    hot_brick = jax.random.randint(jax.random.fold_in(base_key, 1), (), 0, BRICKS, dtype=jnp.int32)
    block_keys = jax.random.split(jax.random.fold_in(base_key, 2), BRICKS)
    blocks = jax.vmap(brick_block, in_axes=(0, None))(block_keys, hot_brick)
    return blocks.reshape(-1).astype(jnp.int32)


def inverse_table(table_key):
    diag_key, off_key = jax.random.split(table_key)
    diagonal = jax.random.uniform(diag_key, (BTYPES, COND), jnp.float32, 0.8, 1.2)
    offdiag = jnp.clip(0.1 * jax.random.normal(off_key, (BTYPES, COND, COND), jnp.float32), -0.2, 0.2)
    offdiag = 0.5 * (offdiag + jnp.swapaxes(offdiag, 1, 2))
    identity = jnp.eye(COND, dtype=jnp.float32)
    return offdiag * (1.0 - identity) + identity * diagonal[:, :, None]


def draw_inv_induct(key, part):
    return inverse_table(jax.random.fold_in(key, 101))


def draw_inv_capac(key, part):
    return inverse_table(jax.random.fold_in(key, 202))


def set_ends(values, own_key, least, high):
    longest = values.shape.index(max(values.shape))
    spots = []
    for shift in (0, 1):
        where = [jax.random.randint(jax.random.fold_in(own_key, axis), (), 0, length) for axis, length in enumerate(values.shape)]
        where[longest] = (where[longest] + shift) % values.shape[longest]
        spots.append(tuple(where))
    return values.at[spots[0]].set(least).at[spots[1]].set(high)


def levels(stream_key, dims, shards, low, largest):
    loudness, own = 1.0, jax.random.fold_in(stream_key, 6)
    for dim, shards_of in shards:
        draws = jnp.exp(jax.random.uniform(jax.random.fold_in(own, dim), (shards_of,), jnp.float32, low / len(shards), largest / len(shards)))
        loudness = loudness * jnp.repeat(draws, dims[dim] // shards_of).reshape([-1 if axis == dim else 1 for axis in range(len(dims))])
    return loudness


def split_up(number_of, total, reach, slope):
    loads = [(1 << 20) // math.isqrt(standing ** slope) + 1 for standing in range(2, number_of + 1)]
    rest, holding = total - reach - (number_of - 1), [1] * (number_of - 1)
    while rest > 0:
        movable = [i for i in range(number_of - 1) if holding[i] < reach]
        mass, left = sum([loads[i] for i in movable]), rest
        for i in movable:
            addition = min(reach - holding[i], max(1, left * loads[i] // mass), rest)
            holding[i] = holding[i] + addition
            rest = rest - addition
    return np.array([reach] + holding)


def uneven_parts(key, amount, total, limit, slope):
    if amount == 2:
        one = jax.random.randint(key, (), max(1, total - limit), min(limit, total - 1) + 1)
        return jnp.stack([one, total - one])
    sizes = jnp.asarray(split_up(amount, total, limit, slope), jnp.int32)
    couples = (amount - 1) // 2
    donor, sink = sizes[1:1 + 2 * couples:2], sizes[2:2 + 2 * couples:2]
    margin = jnp.minimum(donor - 1, limit - sink)
    shifted = jax.random.randint(jax.random.fold_in(key, 1), (couples,), 0, 1 << 20) % (margin + 1)
    sizes = sizes.at[1:1 + 2 * couples:2].set(donor - shifted).at[2:2 + 2 * couples:2].set(sink + shifted)
    return sizes[jax.random.permutation(jax.random.fold_in(key, 2), amount)]


def centred(stream_key, dims, deviation, most, shards=(), held_as=jnp.bfloat16):
    drawn = deviation * jax.random.normal(stream_key, dims, jnp.float32)
    if shards:
        drawn = drawn * levels(stream_key, dims, shards, -0.22, 0.18)
    return jnp.clip(drawn, -most, most).astype(held_as)


def setup_inputs(seed: int = 0) -> dict:
    splits = jax.random.split(jax.random.key(seed), 15)
    e_field = centred(splits[0], (3, NX, NY, NZ), 1.0, 6.0, ((1, 2), (2, 4), (3, 4)), jnp.float32)
    h_field = centred(splits[1], (3, NX, NY, NZ), 1.0, 6.0, ((1, 2), (2, 4), (3, 4)), jnp.float32)
    material = set_ends(jax.random.randint(splits[2], (NX, NY, NZ), 0, MATS), jax.random.fold_in(splits[2], 1), 0, MATS - 1).astype(jnp.int32)
    permittivity = jnp.clip(jnp.exp(jax.random.uniform(splits[3], (MATS,), jnp.float32, math.log(1.0), math.log(10.0))), 1.0, 10.0)
    line_volts = centred(splits[4], (COND, SEGS), 1.0, 6.0, ((1, 32),), jnp.float32)
    line_amps = centred(splits[5], (COND, SEGS), 1.0, 6.0, ((1, 32),), jnp.float32)
    coupling = centred(splits[6], (COND, SEGS), 0.5, 3.0, ((1, 32),), jnp.float32)
    seg_brick = draw_seg_brick(jax.random.fold_in(splits[14], 71), 0)
    seg_cell = set_ends(jax.random.randint(splits[8], (SEGS,), 0, CELLS), jax.random.fold_in(splits[8], 1), 0, CELLS - 1).astype(jnp.int32)
    seg_axis = set_ends(jax.random.randint(splits[9], (SEGS,), 0, 3), jax.random.fold_in(splits[9], 1), 0, 2).astype(jnp.int32)
    bundle_type = set_ends(jax.random.randint(splits[10], (SEGS,), 0, BTYPES), jax.random.fold_in(splits[10], 1), 0, BTYPES - 1).astype(jnp.int32)
    path_lengths = jax.vmap(lambda own: uneven_parts(own, NPATH, S_DEV, PMAX, 1))(jax.random.split(splits[11], BRICKS)).reshape((BRICKS, NPATH)).astype(jnp.int32)
    inv_induct = draw_inv_induct(jax.random.fold_in(splits[14], 71), 0)
    inv_capac = draw_inv_capac(jax.random.fold_in(splits[14], 71), 0)
    return {"e_field": e_field, "h_field": h_field, "material": material, "permittivity": permittivity, "line_volts": line_volts, "line_amps": line_amps, "coupling": coupling, "seg_brick": seg_brick, "seg_cell": seg_cell, "seg_axis": seg_axis, "bundle_type": bundle_type, "path_lengths": path_lengths, "inv_induct": inv_induct, "inv_capac": inv_capac}


courant = 0.5
line_step = 0.5
inject_gain = 0.25


def difference(block, along_dim, keep_lower):
    extent = block.shape[along_dim]
    result = lax.slice_in_dim(block, 1, extent, axis=along_dim) - lax.slice_in_dim(block, 0, extent - 1, axis=along_dim)
    for other_dim in range(3):
        if other_dim != along_dim:
            length = result.shape[other_dim]
            if keep_lower:
                result = lax.slice_in_dim(result, 0, length - 1, axis=other_dim)
            else:
                result = lax.slice_in_dim(result, 1, length, axis=other_dim)
    return result


def curl_of(padded, keep_lower):
    def partial_of(component, along_dim):
        return difference(padded[component], along_dim, keep_lower)
    return jnp.stack([partial_of(2, 1) - partial_of(1, 2), partial_of(0, 2) - partial_of(2, 0), partial_of(1, 0) - partial_of(0, 1)])


def path_masks(lengths_row, count):
    path_ends = jnp.cumsum(lengths_row).astype(jnp.int32)
    path_starts = path_ends - lengths_row.astype(jnp.int32)
    position = jnp.arange(count, dtype=jnp.int32)
    is_last = jnp.any(position[None, :] == (path_ends - 1)[:, None], axis=0)
    is_first = jnp.any(position[None, :] == path_starts[:, None], axis=0)
    return jnp.where(is_last, 0.0, 1.0).astype(jnp.float32), jnp.where(is_first, 0.0, 1.0).astype(jnp.float32)


def line_block(inputs, inv_induct, inv_capac):
    volts_now, amps_now, coupling, tangent, kinds, lengths_row = inputs
    not_last, not_first = path_masks(lengths_row, volts_now.shape[1])
    conductors = volts_now.shape[0]
    ahead = jnp.concatenate([volts_now[:, 1:], jnp.zeros((conductors, 1), jnp.float32)], axis=1) * not_last[None, :]
    drive = ahead - volts_now - coupling * tangent[None, :]
    induct_rows = inv_induct[kinds]
    amps_next = amps_now - line_step * jnp.einsum("sij,js->is", induct_rows, drive, precision=lax.Precision.HIGHEST)
    behind = jnp.concatenate([jnp.zeros((conductors, 1), jnp.float32), amps_next[:, :-1]], axis=1) * not_first[None, :]
    capac_rows = inv_capac[kinds]
    volts_next = volts_now - line_step * jnp.einsum("sij,js->is", capac_rows, amps_next - behind, precision=lax.Precision.HIGHEST)
    return volts_next, amps_next


def reference(e_field, h_field, material, permittivity, line_volts, line_amps, coupling, seg_brick, seg_cell, seg_axis, bundle_type, path_lengths, inv_induct, inv_capac):
    coeff = courant / permittivity[material]
    brick_len = seg_brick // (N_WID * N_HGT)
    brick_wid = (seg_brick // N_HGT) % N_WID
    brick_hgt = seg_brick % N_HGT
    cell_x = (brick_len * CX + seg_cell // (CY * CZ)).astype(jnp.int32)
    cell_y = (brick_wid * CY + (seg_cell // CZ) % CY).astype(jnp.int32)
    cell_z = (brick_hgt * CZ + seg_cell % CZ).astype(jnp.int32)
    conductors = line_volts.shape[0]

    def owner_blocks(values):
        return values.reshape(conductors, BRICKS, S_DEV).transpose(1, 0, 2)

    def whole_rows(blocks):
        return blocks.transpose(1, 0, 2).reshape(conductors, BRICKS * S_DEV)

    coupling_blocks = owner_blocks(coupling)
    kinds_blocks = bundle_type.reshape(BRICKS, S_DEV)

    def one_owner(inputs):
        return line_block(inputs, inv_induct, inv_capac)

    e_now, h_now = e_field, h_field
    volts_now, amps_now = line_volts, line_amps
    for iteration in range(ITERS):
        tangent = e_now[seg_axis, cell_x, cell_y, cell_z]
        volts_blocks, amps_blocks = lax.map(one_owner, (owner_blocks(volts_now), owner_blocks(amps_now), coupling_blocks, tangent.reshape(BRICKS, S_DEV), kinds_blocks, path_lengths))
        volts_now = whole_rows(volts_blocks)
        amps_now = whole_rows(amps_blocks)
        common = inject_gain * jnp.sum(coupling * amps_now, axis=0)
        injected = jnp.zeros_like(e_now).at[seg_axis, cell_x, cell_y, cell_z].add(common)
        padded_e = jnp.pad(e_now, ((0, 0), (0, 1), (0, 1), (0, 1)))
        h_now = h_now - courant * curl_of(padded_e, True)
        padded_h = jnp.pad(h_now, ((0, 0), (1, 0), (1, 0), (1, 0)))
        e_now = e_now + coeff[None] * (curl_of(padded_h, False) - injected)
    return e_now, h_now, volts_now, amps_now
```

```python
import jax
import jax.numpy as jnp
from jax import lax
from jax.sharding import PartitionSpec as P

ITERS = 4
AXES = ("len", "wid", "hgt")

courant = 0.5
line_step = 0.5
inject_gain = 0.25


def halves(values):
    high = lax.reduce_precision(values, exponent_bits=8, mantissa_bits=7)
    low = values - high
    return high.astype(jnp.bfloat16), low.astype(jnp.bfloat16)


def product(a, b, a_dim, b_dim):
    return lax.dot_general(
        a, b, (((a_dim,), (b_dim,)), ((), ())), preferred_element_type=jnp.float32
    )


def one_hot(indices, size):
    rows = lax.broadcasted_iota(jnp.int32, (size, indices.shape[0]), 0)
    return rows == indices[None, :]


def ranks_in_brick(in_brick):
    devices, count = in_brick.shape
    grouped = in_brick.astype(jnp.bfloat16).reshape(devices, count // 128, 128)
    lane = jnp.arange(128, dtype=jnp.int32)
    before = (lane[:, None] < lane[None, :]).astype(jnp.bfloat16)
    within = product(grouped, before, 2, 0)
    totals = jnp.sum(grouped.astype(jnp.float32), axis=2)
    block = jnp.arange(count // 128, dtype=jnp.int32)
    earlier = (block[:, None] < block[None, :]).astype(jnp.float32)
    ahead = jnp.sum(totals[:, :, None] * earlier[None], axis=1)
    counts = (within + ahead[:, :, None]).reshape(devices, count)
    return jnp.sum(jnp.where(in_brick, counts, 0.0), axis=0).astype(jnp.int32)


def path_masks(lengths_row, count):
    path_ends = jnp.cumsum(lengths_row)
    path_starts = path_ends - lengths_row
    position = jnp.arange(count, dtype=jnp.int32)
    is_last = jnp.any(position[None, :] == (path_ends - 1)[:, None], axis=0)
    is_first = jnp.any(position[None, :] == path_starts[:, None], axis=0)
    return (
        jnp.where(is_last, 0.0, 1.0).astype(jnp.float32),
        jnp.where(is_first, 0.0, 1.0).astype(jnp.float32),
    )


def type_table(table):
    kinds, rows, columns = table.shape
    flat = jnp.transpose(table, (1, 0, 2)).reshape(rows, kinds * columns)
    high, low = halves(flat)
    return jnp.concatenate(
        [
            jnp.concatenate([high, high], axis=1),
            jnp.concatenate([low, jnp.zeros_like(low)], axis=1),
        ],
        axis=0,
    )


def apply_types(table, operand, kind_hot):
    kinds = kind_hot.shape[0]
    rows, count = operand.shape
    parts = [
        (kind_hot[:, None, :] * part[None]).reshape(kinds * rows, count)
        for part in halves(operand)
    ]
    result = product(table, jnp.concatenate(parts, axis=0), 1, 0)
    return result[:rows] + result[rows:]


def neighbour(block, axis, upward):
    count = lax.axis_size(axis)
    pairs = [(i, i + 1) if upward else (i + 1, i) for i in range(count - 1)]
    return lax.ppermute(block, axis, pairs)


def shards(
    e_field,
    h_field,
    material,
    permittivity,
    line_volts,
    line_amps,
    coupling,
    seg_brick,
    seg_cell,
    seg_axis,
    bundle_type,
    path_lengths,
    inv_induct,
    inv_capac,
):
    devices = lax.axis_size("len") * lax.axis_size("wid") * lax.axis_size("hgt")
    conductors, seg_count = line_volts.shape
    capacity = seg_count // devices * 5 // 2
    rows_x, rows_y, rows_z = e_field.shape[1:]
    rows = 3 * rows_x * rows_y
    coeff = jnp.zeros(material.shape, jnp.float32)
    for material_id in range(permittivity.shape[0]):
        coeff = jnp.where(material == material_id, courant / permittivity[material_id], coeff)

    in_brick = one_hot(seg_brick, devices)
    in_rank = one_hot(ranks_in_brick(in_brick), capacity).astype(jnp.bfloat16)
    row = seg_axis * (rows_x * rows_y) + seg_cell // rows_z
    pieces = (seg_cell % rows_z + 1, row % 256, row // 256)
    placed = jnp.concatenate([jnp.where(in_brick, piece[None, :], 0) for piece in pieces], axis=0)
    placed = product(placed.astype(jnp.bfloat16), in_rank, 1, 1).astype(jnp.int32)
    wanted = (
        placed[:devices] + placed[devices : 2 * devices] * 256 + placed[2 * devices :] * 65536
    )
    asked = lax.all_to_all(wanted, AXES, split_axis=0, concat_axis=0, tiled=True)
    asked = asked.reshape(devices * capacity)
    row_hot = one_hot(asked // 256, rows).astype(jnp.bfloat16)
    z_hot = one_hot(asked % 256 - 1, rows_z)
    brick_hot = in_brick.astype(jnp.bfloat16)
    brick_hot3 = jnp.concatenate([brick_hot] * 2, axis=0)
    kind_hot = one_hot(bundle_type, inv_induct.shape[0]).astype(jnp.bfloat16)
    induct_table, capac_table = type_table(inv_induct), type_table(inv_capac)
    not_last, not_first = path_masks(path_lengths[0], seg_count)

    e_now, h_now = e_field, h_field
    volts, amps = line_volts, line_amps
    edge = jnp.zeros((conductors, 1), jnp.float32)
    for _ in range(ITERS):
        e_parts = jnp.concatenate(halves(e_now.reshape(rows, rows_z)), axis=1)
        found = product(e_parts, row_hot, 0, 0)
        samples = jnp.sum(jnp.where(z_hot, found[:rows_z] + found[rows_z:], 0.0), axis=0)
        samples = samples.reshape(devices, capacity)
        returned = lax.all_to_all(samples, AXES, split_axis=0, concat_axis=0, tiled=True)

        e_x = jnp.concatenate([e_now, neighbour(e_now[:, :1], "len", False)], axis=1)
        e_y = jnp.concatenate([e_now, neighbour(e_now[:, :, :1], "wid", False)], axis=2)
        e_z = jnp.concatenate([e_now, neighbour(e_now[:, :, :, :1], "hgt", False)], axis=3)
        d_x = e_x[:, 1:] - e_now
        d_y = e_y[:, :, 1:] - e_now
        d_z = e_z[:, :, :, 1:] - e_now
        h_now = h_now - courant * jnp.stack(
            [d_y[2] - d_z[1], d_z[0] - d_x[2], d_x[1] - d_y[0]]
        )
        h_x = jnp.concatenate([neighbour(h_now[:, -1:], "len", True), h_now], axis=1)
        h_y = jnp.concatenate([neighbour(h_now[:, :, -1:], "wid", True), h_now], axis=2)
        h_z = jnp.concatenate([neighbour(h_now[:, :, :, -1:], "hgt", True), h_now], axis=3)
        d_x = h_now - h_x[:, :-1]
        d_y = h_now - h_y[:, :, :-1]
        d_z = h_now - h_z[:, :, :, :-1]
        curl_h = jnp.stack([d_y[2] - d_z[1], d_z[0] - d_x[2], d_x[1] - d_y[0]])

        by_rank = product(jnp.concatenate(halves(returned), axis=0), brick_hot3, 0, 0)
        tangent = jnp.sum(jnp.where(in_rank > 0, by_rank, 0.0), axis=0)
        ahead = jnp.concatenate([volts[:, 1:], edge], axis=1) * not_last[None, :]
        drive = ahead - volts - coupling * tangent[None, :]
        amps = amps - line_step * apply_types(induct_table, drive, kind_hot)
        behind = jnp.concatenate([edge, amps[:, :-1]], axis=1) * not_first[None, :]
        volts = volts - line_step * apply_types(capac_table, amps - behind, kind_hot)
        common = inject_gain * jnp.sum(coupling * amps, axis=0)
        weighed = jnp.concatenate([brick_hot * part[None, :] for part in halves(common)], axis=0)
        outgoing = product(weighed, in_rank, 1, 1)
        outgoing = outgoing[:devices] + outgoing[devices:]
        arrived = lax.all_to_all(outgoing, AXES, split_axis=0, concat_axis=0, tiled=True)
        arrived = arrived.reshape(devices * capacity)
        z_parts = [
            jnp.where(z_hot, part[None, :], jnp.zeros((), jnp.bfloat16)) for part in halves(arrived)
        ]
        injected = product(row_hot, jnp.concatenate(z_parts, axis=0), 1, 1)
        injected = (injected[:, :rows_z] + injected[:, rows_z:]).reshape(e_now.shape)
        e_now = e_now + coeff[None] * (curl_h - injected)
    return (e_now, h_now, volts, amps)


def solution(mesh):
    return jax.shard_map(
        shards,
        mesh=mesh,
        in_specs=(
            P(None, "len", "wid", "hgt"),
            P(None, "len", "wid", "hgt"),
            P("len", "wid", "hgt"),
            P(),
            P(None, ("len", "wid", "hgt")),
            P(None, ("len", "wid", "hgt")),
            P(None, ("len", "wid", "hgt")),
            P(("len", "wid", "hgt")),
            P(("len", "wid", "hgt")),
            P(("len", "wid", "hgt")),
            P(("len", "wid", "hgt")),
            P(("len", "wid", "hgt"), None),
            P(),
            P(),
        ),
        out_specs=(
            P(None, "len", "wid", "hgt"),
            P(None, "len", "wid", "hgt"),
            P(None, ("len", "wid", "hgt")),
            P(None, ("len", "wid", "hgt")),
        ),
        check_vma=False,
    )
```

```python
import functools

import jax
import jax.numpy as jnp
from jax import lax
from jax.experimental import pallas as pl
from jax.experimental.pallas import tpu as pltpu
from jax.sharding import PartitionSpec as P

ITERS = 4
AXES = ("len", "wid", "hgt")

courant = 0.5
line_step = 0.5
inject_gain = 0.25


def halves(values):
    high = lax.reduce_precision(values, exponent_bits=8, mantissa_bits=7)
    low = values - high
    return high.astype(jnp.bfloat16), low.astype(jnp.bfloat16)


def product(a, b, a_dim, b_dim):
    return lax.dot_general(
        a, b, (((a_dim,), (b_dim,)), ((), ())), preferred_element_type=jnp.float32
    )


def one_hot(indices, size):
    rows = lax.broadcasted_iota(jnp.int32, (size, indices.shape[0]), 0)
    return rows == indices[None, :]


def ranks_in_brick(in_brick):
    devices, count = in_brick.shape
    grouped = in_brick.astype(jnp.bfloat16).reshape(devices, count // 128, 128)
    lane = jnp.arange(128, dtype=jnp.int32)
    before = (lane[:, None] < lane[None, :]).astype(jnp.bfloat16)
    within = product(grouped, before, 2, 0)
    totals = jnp.sum(grouped.astype(jnp.float32), axis=2)
    block = jnp.arange(count // 128, dtype=jnp.int32)
    earlier = (block[:, None] < block[None, :]).astype(jnp.float32)
    ahead = jnp.sum(totals[:, :, None] * earlier[None], axis=1)
    counts = (within + ahead[:, :, None]).reshape(devices, count)
    return jnp.sum(jnp.where(in_brick, counts, 0.0), axis=0).astype(jnp.int32)


def path_masks(lengths_row, count):
    path_ends = jnp.cumsum(lengths_row)
    path_starts = path_ends - lengths_row
    position = jnp.arange(count, dtype=jnp.int32)
    is_last = jnp.any(position[None, :] == (path_ends - 1)[:, None], axis=0)
    is_first = jnp.any(position[None, :] == path_starts[:, None], axis=0)
    return (
        jnp.where(is_last, 0.0, 1.0).astype(jnp.float32),
        jnp.where(is_first, 0.0, 1.0).astype(jnp.float32),
    )


def type_table(table):
    kinds, rows, columns = table.shape
    flat = jnp.transpose(table, (1, 0, 2)).reshape(rows, kinds * columns)
    high, low = halves(flat)
    return jnp.concatenate(
        [
            jnp.concatenate([high, high], axis=1),
            jnp.concatenate([low, jnp.zeros_like(low)], axis=1),
        ],
        axis=0,
    )


MESH = pl.DeviceIdType.MESH
CHUNK = 512


def split(values):
    high = values.astype(jnp.bfloat16)
    return high, (values - high.astype(jnp.float32)).astype(jnp.bfloat16)


def apply_types(table, operand, kind_mask):
    parts = [
        jnp.concatenate([part] * (kind_mask.shape[0] // operand.shape[0]), axis=0) * kind_mask
        for part in split(operand)
    ]
    result = product(table, jnp.concatenate(parts, axis=0), 1, 0)
    return result[: operand.shape[0]] + result[operand.shape[0] :]


def kernel(
    sizes,
    full,
    group,
    e_in,
    h_in,
    coeff,
    rows_of,
    z_of,
    brick_hot,
    pos_hot,
    kind_mask,
    not_last,
    not_first,
    volts_in,
    amps_in,
    coupling,
    induct_table,
    capac_table,
    e_out,
    h_out,
    volts,
    amps,
    e_all,
    h_all,
    row_hot,
    e_turned,
    z_parts,
    flat,
    sample_send,
    sample_recv,
    drive_send,
    drive_recv,
    ey_send,
    ey_halo,
    ez_send,
    ez_halo,
    hy_send,
    hy_halo,
    hz_send,
    hz_halo,
    face_send_sem,
    face_recv_sem,
    a2a_send_sem,
    a2a_recv_sem,
):
    axes = ("len", "wid", "hgt")
    place = [lax.axis_index(axis) for axis in axes]
    me = (place[0] * sizes[1] + place[1]) * sizes[2] + place[2]
    devices = sizes[0] * sizes[1] * sizes[2]
    _, rows_x, rows_y, rows_z = e_in.shape
    rows = 3 * rows_x * rows_y
    slots = rows_of.shape[1]
    conductors, count = volts.shape

    def device(number):
        upper = lax.div(number, sizes[2])
        return (lax.div(upper, sizes[1]), lax.rem(upper, sizes[1]), lax.rem(number, sizes[2]))

    for halo in (ey_halo, ez_halo, hy_halo, hz_halo):
        halo[...] = jnp.zeros(halo.shape, jnp.float32)
    e_all[:, rows_x] = jnp.zeros((3, rows_y, rows_z), jnp.float32)
    h_all[:, 0] = jnp.zeros((3, rows_y, rows_z), jnp.float32)

    barrier = pltpu.get_barrier_semaphore()

    def greet(step, carry):
        other = lax.rem(me + step, devices)
        pl.semaphore_signal(barrier, inc=1, device_id=device(other), device_id_type=MESH)
        return carry

    lax.fori_loop(1, devices, greet, 0)

    e_all[:, :rows_x] = e_in[...]
    h_all[:, 1:] = h_in[...]
    volts[...] = volts_in[...]
    amps[...] = amps_in[...]

    def mark(step, carry):
        base = pl.multiple_of(step * 16, 16)
        number = lax.broadcasted_iota(jnp.int32, (16, CHUNK), 0) + base
        for start in range(0, slots, CHUNK):
            hit = rows_of[:, start : start + CHUNK] == number
            row_hot[pl.ds(base, 16), start : start + CHUNK] = jnp.where(hit, 1.0, 0.0).astype(
                jnp.bfloat16
            )
        return carry

    lax.fori_loop(0, rows // 16, mark, 0)
    pl.semaphore_wait(barrier, devices - 1)

    def faces(sources, targets, upward, first_sem):
        found = []
        for axis in range(3):
            target = list(place)
            if upward:
                has_next, has_previous = place[axis] < sizes[axis] - 1, place[axis] > 0
                target[axis] = jnp.minimum(place[axis] + 1, sizes[axis] - 1)
            else:
                has_next, has_previous = place[axis] > 0, place[axis] < sizes[axis] - 1
                target[axis] = jnp.maximum(place[axis] - 1, 0)
            copy = pltpu.make_async_remote_copy(
                src_ref=sources[axis],
                dst_ref=targets[axis],
                send_sem=face_send_sem.at[first_sem + axis],
                recv_sem=face_recv_sem.at[first_sem + axis],
                device_id=tuple(target),
                device_id_type=MESH,
            )
            found.append((copy, has_next, has_previous))
        return found

    def start_faces(copies):
        for copy, has_next, _ in copies:
            pl.when(has_next)(copy.start)

    def finish_sends(copies):
        for copy, has_next, _ in copies:
            pl.when(has_next)(copy.wait_send)

    def finish_recvs(copies):
        for copy, _, has_previous in copies:
            pl.when(has_previous)(copy.wait_recv)

    e_copies = faces(
        (e_all.at[pl.ds(1, 2), 0], ey_send, ez_send),
        (e_all.at[pl.ds(1, 2), rows_x], ey_halo, ez_halo),
        False,
        0,
    )
    h_copies = faces(
        (h_all.at[pl.ds(1, 2), rows_x], hy_send, hz_send),
        (h_all.at[pl.ds(1, 2), 0], hy_halo, hz_halo),
        True,
        3,
    )

    def exchange(send, recv, which, fill):
        recv[me] = fill(me)

        def one(step, carry):
            other = lax.rem(me + step, devices)
            send[other] = fill(other)
            pltpu.make_async_remote_copy(
                src_ref=send.at[other],
                dst_ref=recv.at[me],
                send_sem=a2a_send_sem.at[which],
                recv_sem=a2a_recv_sem.at[which],
                device_id=device(other),
                device_id_type=MESH,
            ).start()
            return carry

        lax.fori_loop(1, devices, one, 0)

    def arrivals(ref, sem):
        view = ref.at[pl.ds(0, devices - 1)]
        pltpu.make_async_copy(view, view, sem).wait()

    lane = lax.broadcasted_iota(jnp.int32, (rows_y, rows_z), 1)
    line = lax.broadcasted_iota(jnp.int32, (rows_y, rows_z), 0)

    def pack(ref, first, index, source_lane):
        packed = jnp.zeros((rows_y, rows_z), jnp.float32)
        for comp in range(2):
            for i in range(rows_x):
                spot = comp * rows_x + i
                turned = pltpu.roll(ref[comp, first + i], (spot - source_lane) % rows_z, 1)
                packed = jnp.where(lane == spot, turned, packed)
        index[...] = packed

    def step(_, carry):
        for comp in range(2):
            for i in range(rows_x):
                ey_send[comp, i : i + 1] = e_all[2 * comp, i, 0:1]
        pack(e_all, 0, ez_send, 0)
        start_faces(e_copies)

        for comp in range(3):
            turned = e_all[comp, :rows_x].reshape(rows_x * rows_y, rows_z).T
            high, low = split(turned)
            at = comp * rows_x * rows_y
            e_turned[:rows_z, at : at + rows_x * rows_y] = high
            e_turned[rows_z:, at : at + rows_x * rows_y] = low

        def find(part, carry):
            at = pl.multiple_of(part * CHUNK, CHUNK)
            found = product(e_turned[...], row_hot[:, pl.ds(at, CHUNK)], 1, 0)
            number = lax.broadcasted_iota(jnp.int32, (rows_z, CHUNK), 0)
            hit = z_of[:, pl.ds(at, CHUNK)] == number
            value = jnp.where(hit, found[:rows_z] + found[rows_z:], 0.0)
            flat[:, pl.ds(at, CHUNK)] = jnp.sum(value, axis=0, keepdims=True)
            return carry

        lax.fori_loop(0, slots // CHUNK, find, 0)

        def samples_for(other):
            numbers = [part * devices + other for part in range(full)]
            if group:
                numbers.append(full * devices + lax.div(other, group))
            found = [flat[:, pl.ds(pl.multiple_of(n * 128, 128), 128)] for n in numbers]
            return jnp.concatenate(found, axis=1)

        exchange(sample_send, sample_recv, 0, samples_for)

        finish_recvs(e_copies)

        def magnetic(i, carry):
            ex, ey, ez = (e_all[comp, i] for comp in range(3))

            def along_y(value, slot):
                row = ey_halo[slot, pl.ds(i, 1)]
                return jnp.where(line == rows_y - 1, row, pltpu.roll(value, rows_y - 1, 0)) - value

            def along_z(value, slot):
                halo = pltpu.roll(ez_halo[...], rows_z - 1 - slot * rows_x - i, 1)
                return jnp.where(lane == rows_z - 1, halo, pltpu.roll(value, rows_z - 1, 1)) - value

            h_all[0, i + 1] = h_all[0, i + 1] - courant * (along_y(ez, 1) - along_z(ey, 1))
            h_all[1, i + 1] = h_all[1, i + 1] - courant * (
                along_z(ex, 0) - (e_all[2, i + 1] - ez)
            )
            h_all[2, i + 1] = h_all[2, i + 1] - courant * (
                (e_all[1, i + 1] - ey) - along_y(ex, 0)
            )
            return carry

        lax.fori_loop(0, rows_x, magnetic, 0)
        for comp in range(2):
            for i in range(rows_x):
                hy_send[comp, i : i + 1] = h_all[2 * comp, i + 1, rows_y - 1 : rows_y]
        pack(h_all, 1, hz_send, rows_z - 1)
        start_faces(h_copies)

        arrivals(sample_recv, a2a_recv_sem.at[0])
        returned = jnp.concatenate(split(sample_recv[:, 0, :]), axis=0)
        tangents = []
        for start in range(0, count, CHUNK):
            hot = brick_hot[:, start : start + CHUNK]
            by_pos = product(returned, jnp.concatenate([hot, hot], axis=0), 0, 0)
            kept = by_pos * pos_hot[:, start : start + CHUNK].astype(jnp.float32)
            tangents.append(jnp.sum(kept, axis=0, keepdims=True))
        tangent = jnp.concatenate(tangents, axis=1)
        now = volts[...]
        ahead = pltpu.roll(now, count - 1, 1) * not_last[...]
        drive = ahead - now - coupling[...] * tangent
        amps_now = amps[...] - line_step * apply_types(induct_table[...], drive, kind_mask[...])
        amps[...] = amps_now
        common = inject_gain * jnp.sum(coupling[...] * amps_now, axis=0, keepdims=True)
        weighed = jnp.concatenate([brick_hot[...] * part for part in split(common)], axis=0)
        outgoing = product(weighed, pos_hot[...], 1, 1)
        finish_sends(e_copies)
        arrivals(sample_send, a2a_send_sem.at[0])
        drive_send[:, 0, :] = outgoing[:devices] + outgoing[devices:]
        exchange(drive_send, drive_recv, 1, lambda other: drive_send[other])

        behind = pltpu.roll(amps_now, 1, 1) * not_first[...]
        volts[...] = now - line_step * apply_types(
            capac_table[...], amps_now - behind, kind_mask[...]
        )

        finish_recvs(h_copies)

        def electric(i, carry):
            hx, hy, hz = (h_all[comp, i + 1] for comp in range(3))

            def along_y(value, slot):
                row = hy_halo[slot, pl.ds(i, 1)]
                return value - jnp.where(line == 0, row, pltpu.roll(value, 1, 0))

            def along_z(value, slot):
                shift = lax.rem(2 * rows_z - slot * rows_x - i, rows_z)
                halo = pltpu.roll(hz_halo[...], shift, 1)
                return value - jnp.where(lane == 0, halo, pltpu.roll(value, 1, 1))

            gain = coeff[i]
            e_all[0, i] = e_all[0, i] + gain * (along_y(hz, 1) - along_z(hy, 1))
            e_all[1, i] = e_all[1, i] + gain * (along_z(hx, 0) - (hz - h_all[2, i]))
            e_all[2, i] = e_all[2, i] + gain * ((hy - h_all[1, i]) - along_y(hx, 0))
            return carry

        lax.fori_loop(0, rows_x, electric, 0)

        arrivals(drive_recv, a2a_recv_sem.at[1])
        number = lax.broadcasted_iota(jnp.int32, (rows_z, 128), 0)
        for block in range(slots // 128):
            if block < full * devices:
                part, other = divmod(block, devices)
                values = drive_recv[other, :, part * 128 : part * 128 + 128]
            else:
                first = (block - full * devices) * group
                values = drive_recv[first, :, full * 128 :]
                for other in range(first + 1, first + group):
                    values = values + drive_recv[other, :, full * 128 :]
            hit = z_of[:, block * 128 : block * 128 + 128] == number
            high, low = split(values)
            for which, part in enumerate((high, low)):
                z_parts[which * rows_z : (which + 1) * rows_z, block * 128 : block * 128 + 128] = (
                    jnp.where(hit, part.astype(jnp.float32), 0.0).astype(jnp.bfloat16)
                )

        def inject(part, carry):
            at = pl.multiple_of(part * rows_y * 8, rows_y * 8)
            added = product(row_hot[pl.ds(at, rows_y * 8)], z_parts[...], 1, 1)
            added = (added[:, :rows_z] + added[:, rows_z:]).reshape(8, rows_y, rows_z)
            comp = lax.div(part, rows_x // 8)
            first = lax.rem(part, rows_x // 8) * 8
            e_all[comp, pl.ds(first, 8)] = (
                e_all[comp, pl.ds(first, 8)] - coeff[pl.ds(first, 8)] * added
            )
            return carry

        lax.fori_loop(0, rows // (rows_y * 8), inject, 0)
        finish_sends(h_copies)
        arrivals(drive_send, a2a_send_sem.at[1])
        return carry

    lax.fori_loop(0, ITERS, step, 0)
    e_out[...] = e_all[:, :rows_x]
    h_out[...] = h_all[:, 1:]


def shards(
    e_field,
    h_field,
    material,
    permittivity,
    line_volts,
    line_amps,
    coupling,
    seg_brick,
    seg_cell,
    seg_axis,
    bundle_type,
    path_lengths,
    inv_induct,
    inv_capac,
):
    sizes = tuple(lax.axis_size(axis) for axis in AXES)
    devices = sizes[0] * sizes[1] * sizes[2]
    me = lax.axis_index(AXES)
    conductors, seg_count = line_volts.shape
    capacity = seg_count // devices * 5 // 2
    full, rest = divmod(capacity, 128)
    share = 1
    while share < rest:
        share *= 2
    group = 128 // share if rest else 0
    width = 128 * (full + (1 if rest else 0))
    rows_x, rows_y, rows_z = e_field.shape[1:]
    rows = 3 * rows_x * rows_y
    coeff = jnp.zeros(material.shape, jnp.float32)
    for material_id in range(permittivity.shape[0]):
        coeff = jnp.where(material == material_id, courant / permittivity[material_id], coeff)

    in_brick = one_hot(seg_brick, devices)
    rank = ranks_in_brick(in_brick)
    pos = rank
    if rest:
        pos = jnp.where(rank >= full * 128, rank + share * (me % group), rank)
    pos_hot = one_hot(pos, width).astype(jnp.bfloat16)
    row = seg_axis * (rows_x * rows_y) + seg_cell // rows_z
    pieces = (seg_cell % rows_z + 1, row % 256, row // 256)
    placed = jnp.concatenate([jnp.where(in_brick, piece[None, :], 0) for piece in pieces], axis=0)
    placed = product(placed.astype(jnp.bfloat16), pos_hot, 1, 1).astype(jnp.int32)
    wanted = (
        placed[:devices] + placed[devices : 2 * devices] * 256 + placed[2 * devices :] * 65536
    )
    asked = lax.all_to_all(wanted, AXES, split_axis=0, concat_axis=0, tiled=True)
    lists = [asked[:, part * 128 : part * 128 + 128] for part in range(full)]
    if rest:
        lists.append(asked[:, full * 128 :].reshape(devices // group, group, 128).sum(axis=1))
    asked = jnp.concatenate(lists, axis=0).reshape(1, -1)
    slots = asked.shape[1]
    kind_mask = jnp.repeat(one_hot(bundle_type, inv_induct.shape[0]), conductors, axis=0)
    not_last, not_first = path_masks(path_lengths[0], seg_count)

    field = (rows_x, rows_y, rows_z)
    swap = pltpu.VMEM((devices, 1, width), jnp.float32)
    y_face = pltpu.VMEM((2, rows_x, rows_z), jnp.float32)
    z_face = pltpu.VMEM((rows_y, rows_z), jnp.float32)
    return tuple(
        pl.pallas_call(
            functools.partial(kernel, sizes, full, group),
            out_shape=[
                jax.ShapeDtypeStruct(e_field.shape, jnp.float32),
                jax.ShapeDtypeStruct(h_field.shape, jnp.float32),
                jax.ShapeDtypeStruct(line_volts.shape, jnp.float32),
                jax.ShapeDtypeStruct(line_amps.shape, jnp.float32),
            ],
            in_specs=[pl.BlockSpec(memory_space=pltpu.VMEM)] * 15,
            out_specs=[pl.BlockSpec(memory_space=pltpu.VMEM)] * 4,
            scratch_shapes=[
                pltpu.VMEM((3, rows_x + 1, rows_y, rows_z), jnp.float32),
                pltpu.VMEM((3, rows_x + 1, rows_y, rows_z), jnp.float32),
                pltpu.VMEM((rows, slots), jnp.bfloat16),
                pltpu.VMEM((2 * rows_z, rows), jnp.bfloat16),
                pltpu.VMEM((2 * rows_z, slots), jnp.bfloat16),
                pltpu.VMEM((1, slots), jnp.float32),
                swap,
                swap,
                swap,
                swap,
                y_face,
                y_face,
                z_face,
                z_face,
                y_face,
                y_face,
                z_face,
                z_face,
                pltpu.SemaphoreType.DMA((6,)),
                pltpu.SemaphoreType.DMA((6,)),
                pltpu.SemaphoreType.DMA((2,)),
                pltpu.SemaphoreType.DMA((2,)),
            ],
            compiler_params=pltpu.CompilerParams(
                collective_id=0, has_side_effects=True, vmem_limit_bytes=56 * 1024 * 1024
            ),
            cost_estimate=pl.CostEstimate(
                flops=32 * rows * slots * rows_z, bytes_accessed=8 * 1024 * 1024, transcendentals=0
            ),
        )(
            e_field,
            h_field,
            coeff,
            asked // 256,
            asked % 256 - 1,
            in_brick.astype(jnp.bfloat16),
            pos_hot,
            kind_mask.astype(jnp.bfloat16),
            not_last[None, :],
            not_first[None, :],
            line_volts,
            line_amps,
            coupling,
            type_table(inv_induct),
            type_table(inv_capac),
        )
    )


def solution(mesh):
    return jax.shard_map(
        shards,
        mesh=mesh,
        in_specs=(
            P(None, "len", "wid", "hgt"),
            P(None, "len", "wid", "hgt"),
            P("len", "wid", "hgt"),
            P(),
            P(None, ("len", "wid", "hgt")),
            P(None, ("len", "wid", "hgt")),
            P(None, ("len", "wid", "hgt")),
            P(("len", "wid", "hgt")),
            P(("len", "wid", "hgt")),
            P(("len", "wid", "hgt")),
            P(("len", "wid", "hgt")),
            P(("len", "wid", "hgt"), None),
            P(),
            P(),
        ),
        out_specs=(
            P(None, "len", "wid", "hgt"),
            P(None, "len", "wid", "hgt"),
            P(None, ("len", "wid", "hgt")),
            P(None, ("len", "wid", "hgt")),
        ),
        check_vma=False,
    )
```

```python
import functools

import jax
import jax.numpy as jnp
from jax import lax
from jax.experimental import pallas as pl
from jax.experimental.pallas import tpu as pltpu
from jax.sharding import PartitionSpec as P

ITERS = 4
AXES = ("len", "wid", "hgt")

courant = 0.5
line_step = 0.5
inject_gain = 0.25


def halves(values):
    high = lax.reduce_precision(values, exponent_bits=8, mantissa_bits=7)
    low = values - high
    return high.astype(jnp.bfloat16), low.astype(jnp.bfloat16)


def product(a, b, a_dim, b_dim):
    return lax.dot_general(
        a, b, (((a_dim,), (b_dim,)), ((), ())), preferred_element_type=jnp.float32
    )


def one_hot(indices, size):
    rows = lax.broadcasted_iota(jnp.int32, (size, indices.shape[0]), 0)
    return rows == indices[None, :]


def ranks_in_brick(in_brick):
    devices, count = in_brick.shape
    grouped = in_brick.astype(jnp.bfloat16).reshape(devices, count // 128, 128)
    lane = jnp.arange(128, dtype=jnp.int32)
    before = (lane[:, None] < lane[None, :]).astype(jnp.bfloat16)
    within = product(grouped, before, 2, 0)
    totals = jnp.sum(grouped.astype(jnp.float32), axis=2)
    block = jnp.arange(count // 128, dtype=jnp.int32)
    earlier = (block[:, None] < block[None, :]).astype(jnp.float32)
    ahead = jnp.sum(totals[:, :, None] * earlier[None], axis=1)
    counts = (within + ahead[:, :, None]).reshape(devices, count)
    return jnp.sum(jnp.where(in_brick, counts, 0.0), axis=0).astype(jnp.int32)


def path_masks(lengths_row, count):
    path_ends = jnp.cumsum(lengths_row)
    path_starts = path_ends - lengths_row
    position = jnp.arange(count, dtype=jnp.int32)
    is_last = jnp.any(position[None, :] == (path_ends - 1)[:, None], axis=0)
    is_first = jnp.any(position[None, :] == path_starts[:, None], axis=0)
    return (
        jnp.where(is_last, 0.0, 1.0).astype(jnp.float32),
        jnp.where(is_first, 0.0, 1.0).astype(jnp.float32),
    )


def type_table(table):
    kinds, rows, columns = table.shape
    flat = jnp.transpose(table, (1, 0, 2)).reshape(rows, kinds * columns)
    high, low = halves(flat)
    return jnp.concatenate(
        [
            jnp.concatenate([high, high], axis=1),
            jnp.concatenate([low, jnp.zeros_like(low)], axis=1),
        ],
        axis=0,
    )


MESH = pl.DeviceIdType.MESH
CHUNK = 512
FOLD = 1
INJECT = 1


def split(values):
    high = values.astype(jnp.bfloat16)
    return high, (values - high.astype(jnp.float32)).astype(jnp.bfloat16)


def apply_types(table, operand, kind_mask):
    parts = [
        jnp.concatenate([part] * (kind_mask.shape[0] // operand.shape[0]), axis=0) * kind_mask
        for part in split(operand)
    ]
    result = product(table, jnp.concatenate(parts, axis=0), 1, 0)
    return result[: operand.shape[0]] + result[operand.shape[0] :]


def kernel(
    sizes,
    full,
    group,
    e_in,
    h_in,
    material,
    gains,
    wanted,
    brick_hot,
    pos_hot,
    kind_mask,
    not_last,
    not_first,
    volts_in,
    amps_in,
    coupling,
    induct_table,
    capac_table,
    e_out,
    h_out,
    volts,
    amps,
    e_all,
    h_all,
    coeff,
    rows_of,
    z_of,
    row_hot,
    e_turned,
    z_parts,
    flat,
    sample_send,
    sample_recv,
    drive_send,
    drive_recv,
    ey_send,
    ey_halo,
    ez_send,
    ez_halo,
    hy_send,
    hy_halo,
    hz_send,
    hz_halo,
    face_send_sem,
    face_recv_sem,
    a2a_send_sem,
    a2a_recv_sem,
):
    axes = ("len", "wid", "hgt")
    place = [lax.axis_index(axis) for axis in axes]
    me = (place[0] * sizes[1] + place[1]) * sizes[2] + place[2]
    devices = sizes[0] * sizes[1] * sizes[2]
    _, rows_x, rows_y, rows_z = e_in.shape
    rows, slots = row_hot.shape
    span_x = rows_x // FOLD
    deep = FOLD * rows_z
    conductors, count = volts.shape

    def device(number):
        upper = lax.div(number, sizes[2])
        return (lax.div(upper, sizes[1]), lax.rem(upper, sizes[1]), lax.rem(number, sizes[2]))

    for halo in (ey_halo, ez_halo, hy_halo, hz_halo):
        halo[...] = jnp.zeros(halo.shape, jnp.float32)
    e_all[:, rows_x] = jnp.zeros((3, rows_y, rows_z), jnp.float32)
    h_all[:, 0] = jnp.zeros((3, rows_y, rows_z), jnp.float32)

    barrier = pltpu.get_barrier_semaphore()

    def greet(step, carry):
        other = lax.rem(me + step, devices)
        pl.semaphore_signal(barrier, inc=1, device_id=device(other), device_id_type=MESH)
        return carry

    lax.fori_loop(1, devices, greet, 0)

    def faces(sources, targets, upward, first_sem):
        found = []
        for axis in range(3):
            target = list(place)
            if upward:
                has_next, has_previous = place[axis] < sizes[axis] - 1, place[axis] > 0
                target[axis] = jnp.minimum(place[axis] + 1, sizes[axis] - 1)
            else:
                has_next, has_previous = place[axis] > 0, place[axis] < sizes[axis] - 1
                target[axis] = jnp.maximum(place[axis] - 1, 0)
            copy = pltpu.make_async_remote_copy(
                src_ref=sources[axis],
                dst_ref=targets[axis],
                send_sem=face_send_sem.at[first_sem + axis],
                recv_sem=face_recv_sem.at[first_sem + axis],
                device_id=tuple(target),
                device_id_type=MESH,
            )
            found.append((copy, has_next, has_previous))
        return found

    def start_faces(copies):
        for copy, has_next, _ in copies:
            pl.when(has_next)(copy.start)

    def finish_sends(copies):
        for copy, has_next, _ in copies:
            pl.when(has_next)(copy.wait_send)

    def finish_recvs(copies):
        for copy, _, has_previous in copies:
            pl.when(has_previous)(copy.wait_recv)

    e_copies = faces(
        (e_all.at[pl.ds(1, 2), 0], ey_send, ez_send),
        (e_all.at[pl.ds(1, 2), rows_x], ey_halo, ez_halo),
        False,
        0,
    )
    h_copies = faces(
        (h_all.at[pl.ds(1, 2), rows_x], hy_send, hz_send),
        (h_all.at[pl.ds(1, 2), 0], hy_halo, hz_halo),
        True,
        3,
    )

    def exchange(send, recv, which, fill):
        recv[me] = fill(me)

        def one(step, carry):
            other = lax.rem(me + step, devices)
            send[other] = fill(other)
            pltpu.make_async_remote_copy(
                src_ref=send.at[other],
                dst_ref=recv.at[me],
                send_sem=a2a_send_sem.at[which],
                recv_sem=a2a_recv_sem.at[which],
                device_id=device(other),
                device_id_type=MESH,
            ).start()
            return carry

        lax.fori_loop(1, devices, one, 0)

    def arrivals(ref, sem):
        view = ref.at[pl.ds(0, devices - 1)]
        pltpu.make_async_copy(view, view, sem).wait()

    lane = lax.broadcasted_iota(jnp.int32, (rows_y, rows_z), 1)
    line = lax.broadcasted_iota(jnp.int32, (rows_y, rows_z), 0)

    def pack(ref, first, index, source_lane):
        packed = jnp.zeros((rows_y, rows_z), jnp.float32)
        for comp in range(2):
            for i in range(rows_x):
                spot = comp * rows_x + i
                turned = pltpu.roll(ref[comp, first + i], (spot - source_lane) % rows_z, 1)
                packed = jnp.where(lane == spot, turned, packed)
        index[...] = packed

    def block_values(ref, block):
        if block < full * devices:
            part, other = divmod(block, devices)
            return ref[other, :, part * 128 : part * 128 + 128]
        first = (block - full * devices) * group
        values = ref[first, :, full * 128 :]
        for other in range(first + 1, first + group):
            values = values + ref[other, :, full * 128 :]
        return values

    pl.semaphore_wait(barrier, devices - 1)
    exchange(drive_send, drive_recv, 1, lambda other: wanted[other])

    e_all[:, :rows_x] = e_in[...]
    h_all[:, 1:] = h_in[...]
    volts[...] = volts_in[...]
    amps[...] = amps_in[...]

    def fill_coeff(i, carry):
        kinds = material[i]
        gain = jnp.zeros((rows_y, rows_z), jnp.float32)
        for kind in range(gains.shape[0]):
            gain = jnp.where(kinds == kind, gains[kind : kind + 1], gain)
        coeff[i] = gain
        return carry

    lax.fori_loop(0, rows_x, fill_coeff, 0)
    arrivals(drive_recv, a2a_recv_sem.at[1])
    for block in range(slots // 128):
        code = block_values(drive_recv, block).astype(jnp.int32) - 1
        rows_of[:, block * 128 : block * 128 + 128] = code >> (deep.bit_length() - 1)
        z_of[:, block * 128 : block * 128 + 128] = code & (deep - 1)
    arrivals(drive_send, a2a_send_sem.at[1])

    def mark(step, carry):
        base = pl.multiple_of(step * 16, 16)
        number = lax.broadcasted_iota(jnp.int32, (16, CHUNK), 0) + base
        for start in range(0, slots, CHUNK):
            hit = rows_of[:, start : start + CHUNK] == number
            row_hot[pl.ds(base, 16), start : start + CHUNK] = jnp.where(hit, 1.0, 0.0).astype(
                jnp.bfloat16
            )
        return carry

    lax.fori_loop(0, rows // 16, mark, 0)

    def step(_, carry):
        for comp in range(2):
            for i in range(rows_x):
                ey_send[comp, i : i + 1] = e_all[2 * comp, i, 0:1]
        pack(e_all, 0, ez_send, 0)
        start_faces(e_copies)

        for comp in range(3):
            for fold in range(FOLD):
                part = e_all[comp, fold * span_x : (fold + 1) * span_x]
                high, low = split(part.reshape(span_x * rows_y, rows_z).T)
                at = comp * span_x * rows_y
                e_turned[fold * rows_z : (fold + 1) * rows_z, at : at + span_x * rows_y] = high
                e_turned[deep + fold * rows_z : deep + (fold + 1) * rows_z, at : at + span_x * rows_y] = low

        def find(part, carry):
            at = pl.multiple_of(part * CHUNK, CHUNK)
            found = product(e_turned[...], row_hot[:, pl.ds(at, CHUNK)], 1, 0)
            number = lax.broadcasted_iota(jnp.int32, (deep, CHUNK), 0)
            hit = z_of[:, pl.ds(at, CHUNK)] == number
            value = jnp.where(hit, found[:deep] + found[deep:], 0.0)
            flat[:, pl.ds(at, CHUNK)] = jnp.sum(value, axis=0, keepdims=True)
            return carry

        lax.fori_loop(0, slots // CHUNK, find, 0)

        def samples_for(other):
            numbers = [part * devices + other for part in range(full)]
            if group:
                numbers.append(full * devices + lax.div(other, group))
            found = [flat[:, pl.ds(pl.multiple_of(n * 128, 128), 128)] for n in numbers]
            return jnp.concatenate(found, axis=1)

        exchange(sample_send, sample_recv, 0, samples_for)

        finish_recvs(e_copies)

        def magnetic(i, carry):
            ex, ey, ez = (e_all[comp, i] for comp in range(3))

            def along_y(value, slot):
                row = ey_halo[slot, pl.ds(i, 1)]
                return jnp.where(line == rows_y - 1, row, pltpu.roll(value, rows_y - 1, 0)) - value

            def along_z(value, slot):
                halo = pltpu.roll(ez_halo[...], rows_z - 1 - slot * rows_x - i, 1)
                return jnp.where(lane == rows_z - 1, halo, pltpu.roll(value, rows_z - 1, 1)) - value

            h_all[0, i + 1] = h_all[0, i + 1] - courant * (along_y(ez, 1) - along_z(ey, 1))
            h_all[1, i + 1] = h_all[1, i + 1] - courant * (
                along_z(ex, 0) - (e_all[2, i + 1] - ez)
            )
            h_all[2, i + 1] = h_all[2, i + 1] - courant * (
                (e_all[1, i + 1] - ey) - along_y(ex, 0)
            )
            return carry

        lax.fori_loop(0, rows_x, magnetic, 0)
        for comp in range(2):
            for i in range(rows_x):
                hy_send[comp, i : i + 1] = h_all[2 * comp, i + 1, rows_y - 1 : rows_y]
        pack(h_all, 1, hz_send, rows_z - 1)
        start_faces(h_copies)

        arrivals(sample_recv, a2a_recv_sem.at[0])
        returned = jnp.concatenate(split(sample_recv[:, 0, :]), axis=0)
        tangents = []
        for start in range(0, count, CHUNK):
            hot = brick_hot[:, start : start + CHUNK]
            by_pos = product(returned, jnp.concatenate([hot, hot], axis=0), 0, 0)
            kept = by_pos * pos_hot[:, start : start + CHUNK].astype(jnp.float32)
            tangents.append(jnp.sum(kept, axis=0, keepdims=True))
        tangent = jnp.concatenate(tangents, axis=1)
        now = volts[...]
        ahead = pltpu.roll(now, count - 1, 1) * not_last[...]
        drive = ahead - now - coupling[...] * tangent
        amps_now = amps[...] - line_step * apply_types(induct_table[...], drive, kind_mask[...])
        amps[...] = amps_now
        common = inject_gain * jnp.sum(coupling[...] * amps_now, axis=0, keepdims=True)
        weighed = jnp.concatenate([brick_hot[...] * part for part in split(common)], axis=0)
        outgoing = product(weighed, pos_hot[...], 1, 1)
        finish_sends(e_copies)
        arrivals(sample_send, a2a_send_sem.at[0])
        drive_send[:, 0, :] = outgoing[:devices] + outgoing[devices:]
        exchange(drive_send, drive_recv, 1, lambda other: drive_send[other])

        behind = pltpu.roll(amps_now, 1, 1) * not_first[...]
        volts[...] = now - line_step * apply_types(
            capac_table[...], amps_now - behind, kind_mask[...]
        )

        finish_recvs(h_copies)

        def electric(i, carry):
            hx, hy, hz = (h_all[comp, i + 1] for comp in range(3))

            def along_y(value, slot):
                row = hy_halo[slot, pl.ds(i, 1)]
                return value - jnp.where(line == 0, row, pltpu.roll(value, 1, 0))

            def along_z(value, slot):
                shift = lax.rem(2 * rows_z - slot * rows_x - i, rows_z)
                halo = pltpu.roll(hz_halo[...], shift, 1)
                return value - jnp.where(lane == 0, halo, pltpu.roll(value, 1, 1))

            gain = coeff[i]
            e_all[0, i] = e_all[0, i] + gain * (along_y(hz, 1) - along_z(hy, 1))
            e_all[1, i] = e_all[1, i] + gain * (along_z(hx, 0) - (hz - h_all[2, i]))
            e_all[2, i] = e_all[2, i] + gain * ((hy - h_all[1, i]) - along_y(hx, 0))
            return carry

        lax.fori_loop(0, rows_x, electric, 0)

        arrivals(drive_recv, a2a_recv_sem.at[1])
        number = lax.broadcasted_iota(jnp.int32, (deep, 128), 0)
        for block in range(slots // 128):
            values = block_values(drive_recv, block)
            lanes = slice(block * 128, block * 128 + 128)
            hit = z_of[:, lanes] == number
            high, low = split(values)
            z_parts[:deep, lanes] = jnp.where(hit, high.astype(jnp.float32), 0.0).astype(jnp.bfloat16)
            z_parts[deep:, lanes] = jnp.where(hit, low.astype(jnp.float32), 0.0).astype(jnp.bfloat16)

        for first in range(0, rows, rows // INJECT):
            added = product(row_hot[first : first + rows // INJECT], z_parts[...], 1, 1)
            comps = slice(first * 3 // rows, first * 3 // rows + 3 // INJECT)
            for fold in range(FOLD):
                high = added[:, fold * rows_z : (fold + 1) * rows_z]
                low = added[:, deep + fold * rows_z : deep + (fold + 1) * rows_z]
                change = (high + low).reshape(3 // INJECT, span_x, rows_y, rows_z)
                planes = slice(fold * span_x, (fold + 1) * span_x)
                e_all[comps, planes] = e_all[comps, planes] - coeff[planes] * change
        finish_sends(h_copies)
        arrivals(drive_send, a2a_send_sem.at[1])
        return carry

    lax.fori_loop(0, ITERS, step, 0)
    e_out[...] = e_all[:, :rows_x]
    h_out[...] = h_all[:, 1:]


def shards(
    e_field,
    h_field,
    material,
    permittivity,
    line_volts,
    line_amps,
    coupling,
    seg_brick,
    seg_cell,
    seg_axis,
    bundle_type,
    path_lengths,
    inv_induct,
    inv_capac,
):
    sizes = tuple(lax.axis_size(axis) for axis in AXES)
    devices = sizes[0] * sizes[1] * sizes[2]
    me = lax.axis_index(AXES)
    conductors, seg_count = line_volts.shape
    capacity = seg_count // devices * 5 // 2
    full, rest = divmod(capacity, 128)
    share = 1
    while share < rest:
        share *= 2
    group = 128 // share if rest else 0
    width = 128 * (full + (1 if rest else 0))
    rows_x, rows_y, rows_z = e_field.shape[1:]
    in_brick = one_hot(seg_brick, devices)
    rank = ranks_in_brick(in_brick)
    pos = rank
    if rest:
        pos = jnp.where(rank >= full * 128, rank + share * (me % group), rank)
    pos_hot = one_hot(pos, width).astype(jnp.bfloat16)
    y_and_z = rows_y * rows_z
    x_of = seg_cell // y_and_z
    span_x = rows_x // FOLD
    row = (seg_axis * span_x + x_of % span_x) * rows_y + seg_cell % y_and_z // rows_z
    code = (row * FOLD + x_of // span_x) * rows_z + seg_cell % rows_z + 1
    pieces = (code % 256, code // 256 % 256, code // 65536)
    placed = jnp.concatenate([jnp.where(in_brick, piece[None, :], 0) for piece in pieces], axis=0)
    placed = product(placed.astype(jnp.bfloat16), pos_hot, 1, 1)
    wanted = placed[:devices] + placed[devices : 2 * devices] * 256 + placed[2 * devices :] * 65536
    gains = jnp.broadcast_to((courant / permittivity)[:, None], (permittivity.shape[0], rows_z))
    rows = 3 * span_x * rows_y
    slots = 128 * (devices * full + (devices // group if rest else 0))
    kind_mask = jnp.repeat(one_hot(bundle_type, inv_induct.shape[0]), conductors, axis=0)
    not_last, not_first = path_masks(path_lengths[0], seg_count)

    field = (rows_x, rows_y, rows_z)
    swap = pltpu.VMEM((devices, 1, width), jnp.float32)
    y_face = pltpu.VMEM((2, rows_x, rows_z), jnp.float32)
    z_face = pltpu.VMEM((rows_y, rows_z), jnp.float32)
    return tuple(
        pl.pallas_call(
            functools.partial(kernel, sizes, full, group),
            out_shape=[
                jax.ShapeDtypeStruct(e_field.shape, jnp.float32),
                jax.ShapeDtypeStruct(h_field.shape, jnp.float32),
                jax.ShapeDtypeStruct(line_volts.shape, jnp.float32),
                jax.ShapeDtypeStruct(line_amps.shape, jnp.float32),
            ],
            in_specs=[pl.BlockSpec(memory_space=pltpu.VMEM)] * 15,
            out_specs=[pl.BlockSpec(memory_space=pltpu.VMEM)] * 4,
            scratch_shapes=[
                pltpu.VMEM((3, rows_x + 1, rows_y, rows_z), jnp.float32),
                pltpu.VMEM((3, rows_x + 1, rows_y, rows_z), jnp.float32),
                pltpu.VMEM(field, jnp.float32),
                pltpu.VMEM((1, slots), jnp.int32),
                pltpu.VMEM((1, slots), jnp.int32),
                pltpu.VMEM((rows, slots), jnp.bfloat16),
                pltpu.VMEM((2 * FOLD * rows_z, rows), jnp.bfloat16),
                pltpu.VMEM((2 * FOLD * rows_z, slots), jnp.bfloat16),
                pltpu.VMEM((1, slots), jnp.float32),
                swap,
                swap,
                swap,
                swap,
                y_face,
                y_face,
                z_face,
                z_face,
                y_face,
                y_face,
                z_face,
                z_face,
                pltpu.SemaphoreType.DMA((6,)),
                pltpu.SemaphoreType.DMA((6,)),
                pltpu.SemaphoreType.DMA((2,)),
                pltpu.SemaphoreType.DMA((2,)),
            ],
            compiler_params=pltpu.CompilerParams(
                collective_id=0, has_side_effects=True, vmem_limit_bytes=56 * 1024 * 1024
            ),
            cost_estimate=pl.CostEstimate(
                flops=32 * rows * slots * rows_z, bytes_accessed=8 * 1024 * 1024, transcendentals=0
            ),
        )(
            e_field,
            h_field,
            material,
            gains,
            wanted[:, None, :],
            in_brick.astype(jnp.bfloat16),
            pos_hot,
            kind_mask.astype(jnp.bfloat16),
            not_last[None, :],
            not_first[None, :],
            line_volts,
            line_amps,
            coupling,
            type_table(inv_induct),
            type_table(inv_capac),
        )
    )


def solution(mesh):
    return jax.shard_map(
        shards,
        mesh=mesh,
        in_specs=(
            P(None, "len", "wid", "hgt"),
            P(None, "len", "wid", "hgt"),
            P("len", "wid", "hgt"),
            P(),
            P(None, ("len", "wid", "hgt")),
            P(None, ("len", "wid", "hgt")),
            P(None, ("len", "wid", "hgt")),
            P(("len", "wid", "hgt")),
            P(("len", "wid", "hgt")),
            P(("len", "wid", "hgt")),
            P(("len", "wid", "hgt")),
            P(("len", "wid", "hgt"), None),
            P(),
            P(),
        ),
        out_specs=(
            P(None, "len", "wid", "hgt"),
            P(None, "len", "wid", "hgt"),
            P(None, ("len", "wid", "hgt")),
            P(None, ("len", "wid", "hgt")),
        ),
        check_vma=False,
    )
```
